32 devices in a mesh: dp: 8 (over z, core), blk: 4 (over y, x).
Axes of the slice: x: 2, y: 2, z: 4, core: 2. Of those that a mesh axis runs over, the one named last changes fastest.
Arguments:
- tokens: bfloat16 [8, 2048, 1024], P('dp', 'blk'), may hold values from -6 to 6
- cotangent: bfloat16 [8, 2048, 1024], P('dp', 'blk'), may hold values from -6 to 6
- lengths: int32 [8, 16], P('dp'), may hold values from 0 to 2048, as said below
- w_query: bfloat16 [1024, 1024], replicated, may hold values from -0.1875 to 0.1875
- w_key: bfloat16 [1024, 1024], replicated, may hold values from -0.1875 to 0.1875
- w_value: bfloat16 [1024, 1024], replicated, may hold values from -0.1875 to 0.1875
- w_out: bfloat16 [1024, 1024], replicated, may hold values from -0.1875 to 0.1875
- w_up: bfloat16 [1024, 4096], replicated, may hold values from -0.1875 to 0.1875
- w_down: bfloat16 [4096, 1024], replicated, may hold values from -0.09375 to 0.09375
- norm_gain: float32 [4, 1024], replicated, may hold values from 0.1 to 1.9
- norm_bias: float32 [4, 1024], replicated, may hold values from -1.8 to 1.8
Outputs:
- mixed: bfloat16 [8, 2048, 1024], P('dp', 'blk')
- grad_tokens: bfloat16 [8, 2048, 1024], P('dp', 'blk')
- grad_query: float32 [1024, 1024], replicated
- grad_key: float32 [1024, 1024], replicated
- grad_value: float32 [1024, 1024], replicated
- grad_out: float32 [1024, 1024], replicated
- grad_up: float32 [1024, 4096], replicated
- grad_down: float32 [4096, 1024], replicated
- grad_gain: float32 [4, 1024], replicated
- grad_bias: float32 [4, 1024], replicated
The draws below stay inside these ranges and needn't reach their ends.
Inputs may be any that keep to these rules, and one draw needn't show every extreme that they name: `lengths`: A row holds its sequences one after another from slot 0 in the order of its entries, zero entries are unused, every other entry is 128 or more, and the slots after them are padding. Of every four consecutive rows exactly one is a single sequence of 2048 tokens; each other row holds at most 1536 real tokens.
All inputs are finite; a program needn't handle non-finite values.
Results may differ from the reference program's by a relative error of at most 0.02.
Values may be sent and summed in bfloat16 or wider, within the bound.
A program may use at most 256 MiB of HBM per device.

```python
import jax
import jax.numpy as jnp
from jax import lax

D = 1024
HEADS = 16
HEAD = 64
FF = 4096
MINLEN = 128
ROW_LEN = 2048
ROWS = 8
SEGS = 16


def draw_lengths(key, part):
    key = jax.random.fold_in(key, 7)
    first_key, second_key, third_key, fourth_key = jax.random.split(key, 4)
    largest = (ROW_LEN // (4 * MINLEN)).bit_length() - 1
    first_exp = jax.random.randint(first_key, (ROWS, SEGS), 0, largest + 1)
    second_exp = jax.random.randint(second_key, (ROWS, SEGS), 0, largest + 1)
    powers = jnp.left_shift(jnp.ones((ROWS, SEGS), jnp.int32), jnp.minimum(first_exp, second_exp))
    spans = MINLEN * powers
    pieces = spans + jax.random.randint(fourth_key, (ROWS, SEGS), 0, spans)
    running = jnp.cumsum(pieces, axis=1)
    retained = jnp.where(running <= ROW_LEN * 3 // 4, pieces, 0)
    offset = jax.random.randint(third_key, (), 0, 4)
    row_ids = jnp.arange(ROWS)
    whole_row = (row_ids + offset) % 4 == 0
    first_col = jnp.arange(SEGS)[None, :] == 0
    single = jnp.where(first_col, ROW_LEN, 0)
    return jnp.where(whole_row[:, None], single, retained).astype(jnp.int32)


def levels(rng, extent, cuts, smallest, high):
    loudness = 1.0
    for dim, parts in cuts:
        heights = jax.random.uniform(jax.random.fold_in(jax.random.fold_in(rng, 6), dim), (parts,), jnp.float32, smallest / len(cuts), high / len(cuts))
        loudness = loudness * jnp.repeat(jnp.exp(heights), extent[dim] // parts).reshape((-1,) + (1,) * (len(extent) - 1 - dim))
    return loudness


def gaussian(rng, extent, width, limit, cuts=(), held_as=jnp.bfloat16):
    drawn = jax.random.normal(rng, extent, jnp.float32) * width
    if len(cuts) > 0:
        drawn = levels(rng, extent, cuts, -0.22, 0.18) * drawn
    return jnp.clip(drawn, min=-limit, max=limit).astype(held_as)


def setup_inputs(seed: int = 0) -> dict:
    key_of = jax.random.split(jax.random.key(seed), 12)
    return {
        "tokens": gaussian(key_of[0], (ROWS, ROW_LEN, D), 1.0, 6.0, ((0, 8), (1, 4))),
        "cotangent": gaussian(key_of[1], (ROWS, ROW_LEN, D), 1.0, 6.0, ((0, 8), (1, 4))),
        "lengths": draw_lengths(jax.random.fold_in(key_of[11], 71), 0),
        "w_query": gaussian(key_of[3], (D, D), D ** -0.5, 0.1875),
        "w_key": gaussian(key_of[4], (D, D), D ** -0.5, 0.1875),
        "w_value": gaussian(key_of[5], (D, D), D ** -0.5, 0.1875),
        "w_out": gaussian(key_of[6], (D, D), D ** -0.5, 0.1875),
        "w_up": gaussian(key_of[7], (D, FF), D ** -0.5, 0.1875),
        "w_down": gaussian(key_of[8], (FF, D), FF ** -0.5, 0.09375),
        "norm_gain": jnp.clip(1.0 + 0.18 * jax.random.normal(key_of[9], (4, D), jnp.float32), 0.1, 1.9),
        "norm_bias": gaussian(key_of[10], (4, D), 0.3, 1.8, (), jnp.float32),
    }


@jax.custom_vjp
def low(v):
    return lax.optimization_barrier(v.astype(jnp.bfloat16)).astype(jnp.float32)

@jax.custom_vjp
def low_back(v):
    return v

def low_keep(v):
    return (low(v), None)

def low_pass(kept, grad):
    return (grad,)

def back_keep(v):
    return (v, None)

def back_low(kept, grad):
    return (low(grad),)
low.defvjp(low_keep, low_pass)
low_back.defvjp(back_keep, back_low)
EPSILON = 1e-05
MASKED_SCORE = -1e+30
HIGHEST_PRECISION = lax.Precision.HIGHEST

def matmul(left, right):
    return jnp.dot(left, right, precision=HIGHEST_PRECISION)

def normalize(values, norm_scale, norm_shift):
    row_mean = lax.optimization_barrier(jnp.mean(values, axis=-1, keepdims=True))
    centred = values - row_mean
    spread = lax.optimization_barrier(jnp.mean(centred * centred, axis=-1, keepdims=True))
    return centred * lax.rsqrt(spread + EPSILON) * norm_scale + norm_shift

def rotate(values, position):
    head_count = values.shape[-1] // HEAD
    shaped = values.reshape(values.shape[:-1] + (head_count, HEAD))
    half_len = HEAD // 2
    frequency = jnp.exp(-jnp.log(10000.0) * jnp.arange(half_len, dtype=jnp.float32) * 2.0 / HEAD)
    angles = position.astype(jnp.float32)[..., None] * frequency
    cos_part = jnp.cos(angles)[..., None, :]
    sin_part = jnp.sin(angles)[..., None, :]
    first_half = shaped[..., :half_len]
    second_half = shaped[..., half_len:]
    turned = jnp.concatenate([first_half * cos_part - second_half * sin_part, second_half * cos_part + first_half * sin_part], axis=-1)
    return turned.reshape(values.shape)

def layout(seg_ends, slot_ids):
    passed = slot_ids[None, :, None] >= seg_ends[:, None, :]
    segment = lax.optimization_barrier(jnp.sum(passed.astype(jnp.int32), axis=-1)).astype(jnp.int32)
    seg_start = lax.optimization_barrier(jnp.max(jnp.where(passed, seg_ends[:, None, :], 0), axis=-1)).astype(jnp.int32)
    return (segment, slot_ids[None, :] - seg_start, slot_ids[None, :] < seg_ends[:, -1:])

def attend(queries, key_rows, values, segment):
    block_len = min(512, ROW_LEN)
    slot_ids = jnp.arange(ROW_LEN, dtype=jnp.int32)
    score_scale = HEAD ** (-0.5)
    query_heads = queries.reshape(ROW_LEN, HEADS, HEAD)
    key_heads = key_rows.reshape(ROW_LEN, HEADS, HEAD)
    value_heads = values.reshape(ROW_LEN, HEADS, HEAD)

    def one_block(block_start):
        rows_here = lax.dynamic_slice_in_dim(query_heads, block_start, block_len, 0)
        query_slots = block_start + jnp.arange(block_len, dtype=jnp.int32)
        query_segment = lax.dynamic_slice_in_dim(segment, block_start, block_len, 0)
        scores = low_back(jnp.einsum('qhd,khd->hqk', rows_here, key_heads, precision=HIGHEST_PRECISION) * score_scale)
        allowed = (slot_ids[None, :] <= query_slots[:, None]) & (segment[None, :] == query_segment[:, None])
        masked = jnp.where(allowed[None], scores, MASKED_SCORE)
        row_max = lax.optimization_barrier(jnp.max(masked, axis=-1, keepdims=True))
        raised = jnp.where(allowed[None], jnp.exp(masked - row_max), 0.0)
        weights = low(raised / lax.optimization_barrier(jnp.sum(raised, axis=-1, keepdims=True)))
        return jnp.einsum('hqk,khd->qhd', weights, value_heads, precision=HIGHEST_PRECISION)
    starts = jnp.arange(ROW_LEN // block_len, dtype=jnp.int32) * block_len
    return lax.map(jax.checkpoint(one_block), starts).reshape(ROW_LEN, HEADS * HEAD)

def layer_row(inputs, params, segment, position, valid_mask):
    w_query, w_key, w_value, w_out, w_up, w_down, norm_gain, norm_bias = params
    normed = low(normalize(inputs, norm_gain[0], norm_bias[0]))
    queries = low(rotate(low_back(matmul(normed, w_query)), position))
    key_rows = low(rotate(low_back(matmul(normed, w_key)), position))
    values = low(low_back(matmul(normed, w_value)))
    attended = low(low_back(attend(queries, key_rows, values, segment)))
    hidden = inputs + normalize(low_back(matmul(attended, w_out)), norm_gain[1], norm_bias[1])
    inner_in = low(normalize(hidden, norm_gain[2], norm_bias[2]))
    active = low(jax.nn.gelu(low_back(matmul(inner_in, w_up))))
    outer_out = normalize(low_back(matmul(active, w_down)), norm_gain[3], norm_bias[3])
    return (hidden + outer_out) * valid_mask.astype(jnp.float32)[:, None]

def reference(tokens, cotangent, lengths, w_query, w_key, w_value, w_out, w_up, w_down, norm_gain, norm_bias):
    params = (w_query.astype(jnp.float32), w_key.astype(jnp.float32), w_value.astype(jnp.float32), w_out.astype(jnp.float32), w_up.astype(jnp.float32), w_down.astype(jnp.float32), norm_gain, norm_bias)
    slot_ids = jnp.arange(ROW_LEN, dtype=jnp.int32)

    def row_step(totals, row_items):
        row_tokens, row_cotangent, row_lengths = row_items
        seg_ends = jnp.cumsum(row_lengths).astype(jnp.int32)[None, :]
        segment, position, valid_mask = layout(seg_ends, slot_ids)

        def forward(inputs, weights):
            return layer_row(inputs, weights, segment[0], position[0], valid_mask[0])
        output, pullback = jax.vjp(forward, row_tokens.astype(jnp.float32), params)
        grad_inputs, grad_params = pullback(row_cotangent.astype(jnp.float32))
        totals = jax.tree.map(lambda running, addition: running + addition, totals, grad_params)
        return (totals, (output.astype(jnp.bfloat16), grad_inputs.astype(jnp.bfloat16)))
    initial = jax.tree.map(jnp.zeros_like, params)
    summed, (mixed, grad_tokens) = lax.scan(row_step, initial, (tokens, cotangent, lengths))
    return (mixed, grad_tokens, summed[0], summed[1], summed[2], summed[3], summed[4], summed[5], summed[6], summed[7])
```

```python
import jax
import jax.numpy as jnp
from jax import lax
from jax.experimental import pallas as pl
from jax.experimental.pallas import tpu as pltpu
from jax.sharding import PartitionSpec as P

HEAD = 64


EPSILON = 1e-05
MASKED_SCORE = -1e30


def passed_along(value, axis, steps):
    count = lax.axis_size(axis)
    pairs = [(source, (source + steps) % count) for source in range(count)]
    return lax.ppermute(value, axis, pairs)


def normalize(values, norm_scale, norm_shift):
    row_mean = jnp.mean(values, axis=-1, keepdims=True)
    centred = values - row_mean
    spread = jnp.mean(centred * centred, axis=-1, keepdims=True)
    return centred * lax.rsqrt(spread + EPSILON) * norm_scale + norm_shift


def rotate(values, position):
    head_count = values.shape[-1] // HEAD
    shaped = values.reshape(values.shape[:-1] + (head_count, HEAD))
    half_len = HEAD // 2
    frequency = jnp.exp(-jnp.log(10000.0) * jnp.arange(half_len, dtype=jnp.float32) * 2.0 / HEAD)
    angles = position.astype(jnp.float32)[..., None] * frequency
    cos_part = jnp.cos(angles)[..., None, :]
    sin_part = jnp.sin(angles)[..., None, :]
    first_half = shaped[..., :half_len]
    second_half = shaped[..., half_len:]
    turned = jnp.concatenate(
        [
            first_half * cos_part - second_half * sin_part,
            second_half * cos_part + first_half * sin_part,
        ],
        axis=-1,
    )
    return turned.reshape(values.shape)


def layout(seg_ends, slot_ids):
    passed = slot_ids[None, :, None] >= seg_ends[:, None, :]
    segment = jnp.sum(passed.astype(jnp.int32), axis=-1)
    seg_start = jnp.max(jnp.where(passed, seg_ends[:, None, :], 0), axis=-1)
    return (segment, slot_ids[None, :] - seg_start, slot_ids[None, :] < seg_ends[:, -1:])


def product(left, right):
    return jnp.dot(left, right, preferred_element_type=jnp.float32)


def contract_rows(left, right):
    return lax.dot_general(
        left, right, (((0,), (0,)), ((), ())), preferred_element_type=jnp.float32
    )


def contract_cols(left, right):
    return lax.dot_general(
        left, right, (((1,), (1,)), ((), ())), preferred_element_type=jnp.float32
    )


def stage_partners(n_dp, n_blk):
    dp, blk = lax.axis_index("dp"), lax.axis_index("blk")
    core = dp % 2
    stages = []

    def flipped(value, stride):
        bit = (value // stride) % 2
        return value + stride * (1 - 2 * bit), bit

    other, bit = flipped(dp, 1)
    stages.append(((other, blk), bit))
    blk_bits = n_blk.bit_length() - 1
    for step in range(blk_bits):
        stride = (1 - core) * (1 << step) + core * (1 << (blk_bits - 1 - step))
        other, bit = flipped(blk, stride)
        stages.append(((dp, other), bit))
    for step in range(1, n_dp.bit_length() - 1):
        other, bit = flipped(dp, 1 << step)
        stages.append(((other, blk), bit))
    return stages


class Reducer:
    def __init__(self, stages, jobs, sub, grads, out, acc, recvs, sems):
        self.stages, self.jobs, self.sub = stages, jobs, sub
        self.grads, self.out, self.acc, self.recvs = grads, out, acc, recvs
        self.own_sem, self.place_sem, self.send_sems, self.recv_sems = sems
        self.count = len(stages)
        self.held = [(0, sub)]
        for _, bit in stages:
            low, size = self.held[-1]
            self.held.append((low + bit * (size // 2), size // 2))
        self.ticks = jobs + 2 * self.count

    @staticmethod
    def scratch(count, jobs, sub, width):
        return [
            pltpu.VMEM((jobs, sub // 2, width), jnp.bfloat16),
            [pltpu.VMEM((jobs, sub >> (k + 1), width), jnp.bfloat16) for k in range(count)],
            (
                pltpu.SemaphoreType.DMA,
                pltpu.SemaphoreType.DMA,
                pltpu.SemaphoreType.DMA((2 * count,)),
                pltpu.SemaphoreType.DMA((2 * count, jobs)),
            ),
        ]

    def rows(self, start, size):
        return pl.ds(pl.multiple_of(start, 16), size)

    def scatter_copy(self, k, j):
        partner, bit = self.stages[k]
        low, size = self.held[k]
        half = size // 2
        sent = low + (1 - bit) * half
        if k == 0:
            src = self.grads.at[self.rows(j * self.sub + sent, half)]
        else:
            src = self.acc.at[j, self.rows(sent - self.held[1][0], half)]
        return pltpu.make_async_remote_copy(
            src_ref=src,
            dst_ref=self.recvs[k].at[j],
            send_sem=self.send_sems.at[k],
            recv_sem=self.recv_sems.at[k, j],
            device_id=partner,
            device_id_type=pl.DeviceIdType.MESH,
        )

    def gather_copy(self, k, j):
        partner, _ = self.stages[k]
        low, size = self.held[k + 1]
        there = self.out.at[self.rows(j * self.sub + low, size)]
        here = there
        if k == self.count - 1:
            here = self.acc.at[j, self.rows(low - self.held[1][0], size)]
        return pltpu.make_async_remote_copy(
            src_ref=here,
            dst_ref=there,
            send_sem=self.send_sems.at[self.count + k],
            recv_sem=self.recv_sems.at[self.count + k, j],
            device_id=partner,
            device_id_type=pl.DeviceIdType.MESH,
        )

    def own_copy(self, j):
        low, size = self.held[1]
        return pltpu.make_async_copy(
            self.grads.at[self.rows(j * self.sub + low, size)], self.acc.at[j], self.own_sem
        )

    def place_copy(self, j):
        low, size = self.held[-1]
        return pltpu.make_async_copy(
            self.acc.at[j, self.rows(low - self.held[1][0], size)],
            self.out.at[self.rows(j * self.sub + low, size)],
            self.place_sem,
        )

    def launch(self, copy_of, k, j):
        @pl.when(j >= 1)
        def _():
            copy_of(k, j - 1).wait_send()

        copy_of(k, j).start()

    def step(self, s, j):
        count = self.count
        if s == 0:
            self.own_copy(j).start()
            self.launch(self.scatter_copy, 0, j)
        elif s <= count:
            k = s - 1
            self.scatter_copy(k, j).wait_recv()
            if k == 0:
                self.own_copy(j).wait()
            low, size = self.held[k + 1]
            mine = self.rows(low - self.held[1][0], size)
            total = self.acc[j, mine].astype(jnp.float32) + self.recvs[k][j].astype(jnp.float32)
            self.acc[j, mine] = total.astype(jnp.bfloat16)
            if s < count:
                self.launch(self.scatter_copy, s, j)
            else:
                self.place_copy(j).start()
                self.launch(self.gather_copy, count - 1, j)
        else:
            k = 2 * count - s
            self.gather_copy(k, j).wait_recv()
            if s == count + 1:
                self.place_copy(j).wait()
            if k > 0:
                self.launch(self.gather_copy, k - 1, j)

    def tick(self, t):
        for s in reversed(range(2 * self.count + 1)):
            j = t - s

            @pl.when((j >= 0) & (j < self.jobs))
            def _(s=s, j=j):
                self.step(s, j)

    def finish(self):
        for k in range(self.count):
            self.scatter_copy(k, self.jobs - 1).wait_send()
            self.gather_copy(k, self.jobs - 1).wait_send()


def greet(partners):
    barrier = pltpu.get_barrier_semaphore()
    for partner in partners:
        pl.semaphore_signal(
            barrier, inc=1, device_id=partner, device_id_type=pl.DeviceIdType.MESH
        )
    pl.semaphore_wait(barrier, len(partners))


def reduce_all(grads, n_dp, n_blk):
    total, width = grads.shape
    devices = n_dp * n_blk
    sub = max(512, 16 * devices)
    jobs = total // sub
    count = devices.bit_length() - 1

    def kernel(grads_ref, out_ref, acc, recvs, sems):
        stages = stage_partners(n_dp, n_blk)
        greet([partner for partner, _ in stages])
        reducer = Reducer(stages, jobs, sub, grads_ref, out_ref, acc, recvs, sems)
        lax.fori_loop(0, reducer.ticks, lambda t, c: (reducer.tick(t), c)[1], 0)
        reducer.finish()

    return pl.pallas_call(
        kernel,
        out_shape=jax.ShapeDtypeStruct((total, width), jnp.bfloat16),
        in_specs=[pl.BlockSpec(memory_space=pl.ANY)],
        out_specs=pl.BlockSpec(memory_space=pl.ANY),
        scratch_shapes=Reducer.scratch(count, jobs, sub, width),
        compiler_params=pltpu.CompilerParams(
            collective_id=1, has_side_effects=True, vmem_limit_bytes=60 * 1024 * 1024
        ),
    )(grads)


def shards(
    tokens, cotangent, lengths, w_query, w_key, w_value, w_out, w_up, w_down, norm_gain, norm_bias
):
    row_count, block_len, model_width = tokens.shape
    head_count = model_width // HEAD
    cycle_size = lax.axis_size("blk")
    cycle_index = lax.axis_index("blk")
    score_scale = HEAD ** (-0.5)
    seg_ends = jnp.cumsum(lengths, axis=1)
    offsets = jnp.arange(block_len, dtype=jnp.int32)
    query_slots = cycle_index * block_len + offsets
    query_segment, query_position, valid_mask = layout(seg_ends, query_slots)
    positions = query_position.reshape(-1)
    valid_col = valid_mask.reshape(-1, 1).astype(jnp.float32)
    inputs = tokens.astype(jnp.float32).reshape(-1, model_width)
    normed, first_back = jax.vjp(normalize, inputs, norm_gain[0], norm_bias[0])
    normed_low = normed.astype(jnp.bfloat16)
    query_full, turn_back = jax.vjp(
        lambda values: rotate(values, positions), product(normed_low, w_query)
    )
    key_full = rotate(product(normed_low, w_key), positions)
    query_low = query_full.astype(jnp.bfloat16).reshape(row_count, block_len, head_count, HEAD)
    key_value = jnp.stack(
        [key_full.astype(jnp.bfloat16), product(normed_low, w_value).astype(jnp.bfloat16)]
    ).reshape(2, row_count, block_len, model_width)

    def needed_for(source):
        key_segment = layout(seg_ends, source * block_len + offsets)[0]
        earlier = source <= cycle_index
        return earlier & jnp.any(key_segment[:, -1] >= query_segment[:, 0])

    def block_scores(key_rows, source):
        key_slots = source * block_len + offsets
        key_segment = layout(seg_ends, key_slots)[0]
        allowed = (key_slots[None, None, :] <= query_slots[None, :, None]) & (
            key_segment[:, None, :] == query_segment[:, :, None]
        )
        key_heads = key_rows.reshape(row_count, block_len, head_count, HEAD)
        scores = (
            jnp.einsum("rqhd,rkhd->rhqk", query_low, key_heads, preferred_element_type=jnp.float32)
            * score_scale
        )
        return (scores, allowed[:, None])

    def absorb(running, block_pair, source):

        def absorb_compute(held):
            run_max, run_sum, run_out = held
            scores, allowed = block_scores(block_pair[0], source)
            masked = jnp.where(allowed, scores, MASKED_SCORE)
            new_max = jnp.maximum(run_max, jnp.max(masked, axis=-1))
            raised = jnp.where(allowed, jnp.exp(masked - new_max[..., None]), 0.0)
            decays = jnp.exp(run_max - new_max)
            value_heads = block_pair[1].reshape(row_count, block_len, head_count, HEAD)
            update = jnp.einsum(
                "rhqk,rkhd->rqhd",
                raised.astype(jnp.bfloat16),
                value_heads,
                preferred_element_type=jnp.float32,
            )
            run_out = run_out * jnp.swapaxes(decays, 1, 2)[..., None] + update
            return (new_max, run_sum * decays + jnp.sum(raised, axis=-1), run_out)

        return lax.cond(needed_for(source), absorb_compute, lambda carried: carried, running)

    starting = (
        jnp.full((row_count, head_count, block_len), MASKED_SCORE, jnp.float32),
        jnp.zeros((row_count, head_count, block_len), jnp.float32),
        jnp.zeros((row_count, block_len, head_count, HEAD), jnp.float32),
    )
    running = absorb(starting, key_value, cycle_index)

    def forward_hop(hop, carried):
        state_now, visiting = carried
        visiting = passed_along(visiting, "blk", -1)
        return (absorb(state_now, visiting, jnp.mod(cycle_index + hop, cycle_size)), visiting)

    running, visited = lax.fori_loop(1, cycle_size, forward_hop, (running, key_value))
    run_max, run_sum, run_out = running
    attended_full = run_out / jnp.swapaxes(run_sum, 1, 2)[..., None]
    log_total = run_max + jnp.log(run_sum)
    attended_low = attended_full.astype(jnp.bfloat16).reshape(-1, model_width)
    post_norm, second_back = jax.vjp(
        normalize, product(attended_low, w_out), norm_gain[1], norm_bias[1]
    )
    hidden = inputs + post_norm
    inner_norm, third_back = jax.vjp(normalize, hidden, norm_gain[2], norm_bias[2])
    inner_low = inner_norm.astype(jnp.bfloat16)
    active, gelu_back = jax.vjp(jax.nn.gelu, product(inner_low, w_up))
    active_low = active.astype(jnp.bfloat16)
    outer_norm, fourth_back = jax.vjp(
        normalize, product(active_low, w_down), norm_gain[3], norm_bias[3]
    )
    mixed = ((hidden + outer_norm) * valid_col).astype(jnp.bfloat16).reshape(tokens.shape)
    grad_rows = cotangent.astype(jnp.float32).reshape(-1, model_width) * valid_col
    down_grad, gain_fourth, bias_fourth = fourth_back(grad_rows)
    down_low = down_grad.astype(jnp.bfloat16)
    grad_down_weight = contract_rows(active_low, down_low)
    up_grad = gelu_back(contract_cols(down_low, w_down))[0]
    up_low = up_grad.astype(jnp.bfloat16)
    grad_up_weight = contract_rows(inner_low, up_low)
    inner_grad, gain_third, bias_third = third_back(contract_cols(up_low, w_up))
    hidden_grad = grad_rows + inner_grad
    late_norms = jnp.concatenate([gain_third, gain_fourth, bias_third, bias_fourth])
    proj_grad, gain_second, bias_second = second_back(hidden_grad)
    proj_low = proj_grad.astype(jnp.bfloat16)
    grad_out_weight = contract_rows(attended_low, proj_low)
    attended_grad = (
        contract_cols(proj_low, w_out)
        .astype(jnp.bfloat16)
        .reshape(row_count, block_len, head_count, HEAD)
    )
    delta_rows = jnp.swapaxes(
        jnp.sum(attended_grad.astype(jnp.float32) * attended_full, axis=-1), 1, 2
    )

    def reflect(held, block_pair, source):

        def reflect_compute(inside):
            query_acc, pair_grads = inside
            scores, allowed = block_scores(block_pair[0], source)
            weights = jnp.where(
                allowed,
                jnp.exp(jnp.where(allowed, scores, MASKED_SCORE) - log_total[..., None]),
                0.0,
            )
            key_heads = block_pair[0].reshape(row_count, block_len, head_count, HEAD)
            value_heads = block_pair[1].reshape(row_count, block_len, head_count, HEAD)
            weight_grads = jnp.einsum(
                "rqhd,rkhd->rhqk", attended_grad, value_heads, preferred_element_type=jnp.float32
            )
            score_grads = (weights * (weight_grads - delta_rows[..., None])).astype(jnp.bfloat16)
            query_acc = (
                query_acc
                + jnp.einsum(
                    "rhqk,rkhd->rqhd", score_grads, key_heads, preferred_element_type=jnp.float32
                )
                * score_scale
            )
            key_part = (
                jnp.einsum(
                    "rhqk,rqhd->rkhd", score_grads, query_low, preferred_element_type=jnp.float32
                )
                * score_scale
            )
            value_part = jnp.einsum(
                "rhqk,rqhd->rkhd",
                weights.astype(jnp.bfloat16),
                attended_grad,
                preferred_element_type=jnp.float32,
            )
            pair_grads = pair_grads + jnp.stack([key_part, value_part]).reshape(pair_grads.shape)
            return (query_acc, pair_grads)

        return lax.cond(needed_for(source), reflect_compute, lambda carried: carried, held)

    query_start = jnp.zeros((row_count, block_len, head_count, HEAD), jnp.float32)
    pair_start = jnp.zeros((2, row_count, block_len, model_width), jnp.float32)

    def send_grads(pair_grads):
        return passed_along(pair_grads.astype(jnp.bfloat16), "blk", -1).astype(pair_grads.dtype)

    def backward_hop(hop, carried):
        query_acc, pair_grads, visiting = carried
        query_acc, pair_grads = reflect(
            (query_acc, pair_grads), visiting, jnp.mod(cycle_index + hop, cycle_size)
        )
        visiting = passed_along(visiting, "blk", -1)
        return (query_acc, send_grads(pair_grads), visiting)

    query_acc, pair_grads, visiting = lax.fori_loop(
        0, cycle_size - 1, backward_hop, (query_start, pair_start, key_value)
    )
    query_acc, pair_grads = reflect(
        (query_acc, pair_grads), visiting, jnp.mod(cycle_index - 1, cycle_size)
    )
    own_grads = send_grads(pair_grads)
    query_grad = turn_back(query_acc.reshape(-1, model_width))[0].astype(jnp.bfloat16)
    key_grad = turn_back(own_grads[0].reshape(-1, model_width))[0].astype(jnp.bfloat16)
    value_grad = own_grads[1].reshape(-1, model_width).astype(jnp.bfloat16)
    grad_query_weight = contract_rows(normed_low, query_grad)
    grad_key_weight = contract_rows(normed_low, key_grad)
    grad_value_weight = contract_rows(normed_low, value_grad)
    normed_grad = (
        contract_cols(query_grad, w_query)
        + contract_cols(key_grad, w_key)
        + contract_cols(value_grad, w_value)
    )
    input_grad, gain_first, bias_first = first_back(normed_grad)
    grad_tokens = (hidden_grad + input_grad).astype(jnp.bfloat16).reshape(tokens.shape)
    early_norms = jnp.concatenate([gain_first, gain_second, bias_first, bias_second])
    low_grads = [
        value.astype(jnp.bfloat16).reshape(-1, model_width)
        for value in (
            grad_down_weight,
            jnp.swapaxes(grad_up_weight.reshape(model_width, -1, model_width), 0, 1),
            grad_out_weight,
            grad_query_weight,
            grad_key_weight,
            grad_value_weight,
        )
    ]
    stacked = jnp.concatenate(low_grads)
    summed_rows = reduce_all(stacked, lax.axis_size("dp"), lax.axis_size("blk"))
    norms = lax.psum(jnp.concatenate([early_norms, late_norms]), ("dp", "blk"))
    norm_early = norms[: 4 * model_width].reshape(4, model_width)
    norm_late = norms[4 * model_width :].reshape(4, model_width)
    ff = grad_down_weight.shape[0]
    summed_rows = summed_rows.astype(jnp.float32)
    squares = summed_rows[2 * ff :].reshape(4, model_width, model_width)
    grad_down = summed_rows[:ff]
    grad_up = jnp.swapaxes(
        summed_rows[ff : 2 * ff].reshape(-1, model_width, model_width), 0, 1
    ).reshape(model_width, ff)
    grad_gain = jnp.stack([norm_early[0], norm_early[1], norm_late[0], norm_late[1]])
    grad_bias = jnp.stack([norm_early[2], norm_early[3], norm_late[2], norm_late[3]])
    return (
        mixed,
        grad_tokens,
        squares[1],
        squares[2],
        squares[3],
        squares[0],
        grad_up,
        grad_down,
        grad_gain,
        grad_bias,
    )


def solution(mesh):
    return jax.shard_map(
        shards,
        mesh=mesh,
        in_specs=(
            P("dp", "blk", None),
            P("dp", "blk", None),
            P("dp", None),
            P(),
            P(),
            P(),
            P(),
            P(),
            P(),
            P(),
            P(),
        ),
        out_specs=(
            P("dp", "blk", None),
            P("dp", "blk", None),
            P(),
            P(),
            P(),
            P(),
            P(),
            P(),
            P(),
            P(),
        ),
        check_vma=False,
    )
```
